32 devices in a mesh: row: 16 (over z, y, x), col: 2 (over core).
Axes of the slice: x: 2, y: 2, z: 4, core: 2. Of those that a mesh axis runs over, the one named last changes fastest.
Arguments:
- features: float32 [64, 32768], P(None, ('row', 'col')), may hold values from -12 to 12
- initial: float32 [32768], P(('row', 'col')), may hold values from 0.1 to 90, as said below
Outputs:
- dist: float32 [32768], P(('row', 'col'))
- residuals: float32 [2], replicated
The draws below stay inside these ranges and needn't reach their ends.
Inputs may be any that keep to these rules, and one draw needn't show every extreme that they name: `initial`: positive starting weights of the policies.
All inputs are finite; a program needn't handle non-finite values.
Results may differ from the reference program's by a relative error of at most 0.0003.
Values sent between devices are 32-bit elements; how exact they have to be, the bound alone decides.
A program may use at most 64 MiB of HBM per device.

```python
import math
import jax
import jax.numpy as jnp
from jax import lax

NPOL = 32768
FEAT = 64
ITERS = 2


def draw_features(key, part):
    half_feat = FEAT // 2
    noise_key = jax.random.fold_in(key, 11)
    power_key = jax.random.fold_in(key, 12)
    guard_key = jax.random.fold_in(key, 13)
    noise = jnp.clip(0.5 * jax.random.normal(noise_key, (FEAT, NPOL), jnp.float32), -3.0, 3.0)
    strength = jnp.clip(4.0 * jax.random.normal(power_key, (1, NPOL), jnp.float32), -12.0, 12.0)
    guard = jax.random.uniform(guard_key, (1, NPOL), jnp.float32, 0.75, 1.25)
    return jnp.concatenate([strength, noise[1:half_feat], guard, noise[half_feat + 1:]], axis=0)


def draw_initial(key, part):
    base = jnp.exp(jax.random.uniform(key, (NPOL,), jnp.float32, math.log(0.1), math.log(10.0)))
    ramp = 1.0 + 2.0 * jnp.arange(NPOL, dtype=jnp.float32) / NPOL
    return base * ramp


def setup_inputs(seed: int = 0) -> dict:
    streams_of = jax.random.split(jax.random.key(seed), 3)
    return {
        "features": draw_features(jax.random.fold_in(streams_of[2], 71), 0),
        "initial": draw_initial(jax.random.fold_in(streams_of[2], 71), 0),
    }


intensity = 0.25


def reference(features, initial):
    half_feat = FEAT // 2
    row_side_all = jnp.concatenate([features[half_feat:], -features[:half_feat]], axis=0)
    height = min(512, NPOL)
    row_blocks = NPOL // height
    step_rate = 1.0 / NPOL

    def sweep(weights):
        def one_rows(running, block_index):
            offset = (block_index * height).astype(jnp.int32)
            row_side = lax.dynamic_slice_in_dim(row_side_all, offset, height, 1)
            row_mass = lax.dynamic_slice_in_dim(weights, offset, height, 0)
            payoff = jnp.einsum("kr,kc->rc", row_side, features, precision=lax.Precision.HIGHEST)
            moves = jax.nn.sigmoid(intensity * payoff)
            inflow = jnp.dot(row_mass, moves, precision=lax.Precision.HIGHEST)
            return running + inflow, jnp.sum(moves, axis=1)

        inflow, totals = lax.scan(one_rows, jnp.zeros((NPOL,), jnp.float32), jnp.arange(row_blocks, dtype=jnp.int32))
        return inflow, totals.reshape(NPOL)

    weights = initial / jnp.sum(initial)
    changes = []
    for iteration in range(ITERS):
        inflow, totals = sweep(weights)
        advanced = step_rate * inflow + weights * (1.0 - step_rate * totals)
        normalizer = jnp.sum(advanced)
        updated = advanced / normalizer
        changes.append(jnp.sum(jnp.abs(updated - weights)))
        weights = updated
    return NPOL * weights, jnp.stack(changes)
```

```python
import functools

import jax
import jax.numpy as jnp
from jax import lax
from jax.experimental import pallas as pl
from jax.experimental.pallas import tpu as pltpu
from jax.sharding import PartitionSpec as P

intensity = 0.25
ROW_TILE = 256
MESH_ID = pl.DeviceIdType.MESH
f32, bf16 = jnp.float32, jnp.bfloat16


def split3(x):
    hi = x.astype(bf16).astype(f32)
    mid = (x - hi).astype(bf16).astype(f32)
    return hi, mid, (x - hi - mid).astype(bf16).astype(f32)


def weight_rows(w, count):
    shape = (count, w.shape[1])
    hi, mid, low = (jnp.broadcast_to(v, shape) for v in split3(w))
    at = lax.broadcasted_iota(jnp.int32, shape, 0)
    tail = jnp.where(at == 3, 1.0, 0.0).astype(f32)
    return jnp.where(at == 0, hi, jnp.where(at == 1, mid, jnp.where(at == 2, low, tail)))


def kernel(
    A, B, feat_ref, init_ref, dist_ref, res_ref,
    col_feat, row_feat, col_w, row_w, col_in, row_in, col_out, row_out, grown,
    row_op, col_op, left, right, kept, row_acc, col_acc, scal,
    send_sem, recv_sem, scal_send, scal_recv,
):
    half = feat_ref.shape[0] // 2
    n = feat_ref.shape[1]
    devices = 2 * A * B
    total = n * devices
    row, core = lax.axis_index("row"), lax.axis_index("col")
    me = row * 2 + core
    p, q = lax.div(row, B), lax.rem(row, B)
    tile = min(ROW_TILE, n)
    own = A

    def later(x, y):
        return jnp.where(x > y, 1, 0)

    row_partner = [None] + [(p * B + (q ^ d), core) for d in range(1, B)]
    col_user = [(row, 1 - core)]
    col_owner = [(row, 1 - core)]
    for d in range(1, A):
        other = p ^ d
        col_user.append((other * B + q, core ^ later(p, other)))
        col_owner.append((other * B + q, core ^ later(other, p)))

    def exchange(round_id, row_src, row_dst, col_src, col_dst, col_to):
        copies = {}
        for d in range(max(A, B)):
            for is_row in (False, True):
                if d >= (B if is_row else A) or (is_row and d == 0):
                    continue
                slot = A + d if is_row else d
                copies[is_row, d] = pltpu.make_async_remote_copy(
                    src_ref=row_src(d) if is_row else col_src(d),
                    dst_ref=row_dst(d) if is_row else col_dst(d),
                    send_sem=send_sem.at[round_id, slot],
                    recv_sem=recv_sem.at[round_id, slot],
                    device_id=row_partner[d] if is_row else col_to[d],
                    device_id_type=MESH_ID,
                )
                copies[is_row, d].start()
        return copies

    def scal_copy(round_id, other, slot):
        return pltpu.make_async_remote_copy(
            src_ref=scal.at[round_id, me],
            dst_ref=scal.at[round_id, slot],
            send_sem=scal_send.at[round_id, other],
            recv_sem=scal_recv.at[round_id, slot],
            device_id=(lax.div(other, 2), lax.rem(other, 2)),
            device_id_type=MESH_ID,
        )

    def scal_start(round_id, value):
        scal[round_id, me] = value

        def one(k, carry):
            scal_copy(round_id, lax.rem(me + k, devices), me).start()
            return carry

        lax.fori_loop(1, devices, one, 0)

    def scal_finish(round_id):
        def one(k, carry):
            other = lax.rem(me + k, devices)
            scal_copy(round_id, other, other).wait()
            return carry

        lax.fori_loop(1, devices, one, 0)
        return jnp.sum(scal[round_id], axis=0)

    def lanes(x):
        return jnp.broadcast_to(jnp.sum(x, axis=1, keepdims=True), (1, 128))

    barrier = pltpu.get_barrier_semaphore()

    def greet(k, carry):
        other = lax.rem(me + k, devices)
        pl.semaphore_signal(
            barrier, inc=1, device_id=(lax.div(other, 2), lax.rem(other, 2)), device_id_type=MESH_ID
        )
        return carry

    lax.fori_loop(1, devices, greet, 0)
    pl.semaphore_wait(barrier, devices - 1)

    feats = exchange(
        0, lambda d: feat_ref, lambda d: row_feat.at[d], lambda d: feat_ref, lambda d: col_feat.at[d], col_user
    )
    starts = exchange(
        1, lambda d: init_ref, lambda d: row_w.at[0, d], lambda d: init_ref, lambda d: col_w.at[0, d], col_user
    )
    weights0 = init_ref[...]
    scal_start(0, lanes(weights0))

    row_acc[...] = jnp.zeros_like(row_acc)
    col_acc[...] = jnp.zeros_like(col_acc)

    def prepare_row(slot, f):
        g = jnp.concatenate([f[half:], -f[:half]], axis=0) * (0.5 * intensity)
        hi = g.astype(bf16).astype(f32)
        both = jnp.concatenate([hi, g - hi], axis=0)
        x = both.T.astype(bf16)
        row_op[slot] = jnp.concatenate([x, x], axis=1)

    def prepare_col(slot, f):
        hi = f.astype(bf16)
        low = (f - hi.astype(f32)).astype(bf16)
        col_op[slot] = jnp.concatenate([hi, hi, low, low], axis=0)

    def weigh_row(slot, w):
        left[slot] = weight_rows(w, 16).astype(bf16)

    def weigh_col(slot, w):
        right[slot] = weight_rows(w, 128).T.astype(bf16)

    def unit(first, kept_slot, row_slot, col_slot, scale):
        down = jnp.zeros((16, n), f32)
        for r in range(n // tile):
            at = pl.ds(r * tile, tile)
            if first:
                payoff = jnp.dot(row_op[row_slot, at], col_op[col_slot], preferred_element_type=f32)
                t = jnp.tanh(payoff).astype(bf16)
                kept[kept_slot, at] = t
            else:
                t = kept[kept_slot, at]
            across = jnp.dot(t, right[col_slot], preferred_element_type=f32)
            row_acc[row_slot, at] += scale * across
            down += jnp.dot(left[row_slot, :, r * tile:(r + 1) * tile], t, preferred_element_type=f32)
        col_acc[col_slot] += scale * down

    def units(first, arrive):
        def shell(m, carry):
            arrive(m)

            def one(j, carry):
                dq = jnp.where(j <= m, m, j - m - 1)
                dp = jnp.where(j <= m, j, m)
                own_or_sibling = jnp.where((q ^ dq) > q, 0, own)
                col_slot = jnp.where(dp == 0, own_or_sibling, dp)
                scale = jnp.where(dq + dp == 0, 0.5, 1.0).astype(f32)

                def run():
                    unit(first, dq * A + dp, dq, col_slot, scale)

                if A == B:
                    run()
                else:
                    pl.when((dq < B) & (dp < A))(run)
                return carry

            return lax.fori_loop(0, 2 * m + 1, one, carry)

        lax.fori_loop(0, max(A, B), shell, 0)

    def sibling_unit(first):
        unit(first, A * B, 0, 0, f32(0.5))

    def wait_slot(copies_sem_round, is_row, d, src, dst):
        slot = A + d if is_row else d
        return pltpu.make_async_remote_copy(
            src_ref=src, dst_ref=dst, send_sem=send_sem.at[copies_sem_round, slot],
            recv_sem=recv_sem.at[copies_sem_round, slot], device_id=(row, 1 - core), device_id_type=MESH_ID,
        )

    prepare_row(0, feat_ref[...])
    prepare_col(own, feat_ref[...])
    weigh_row(0, weights0)
    weigh_col(own, weights0)

    def arrive_first(m):
        @pl.when(m < A)
        def _():
            wait_slot(0, False, m, feat_ref, col_feat.at[m]).wait()
            wait_slot(1, False, m, init_ref, col_w.at[0, m]).wait()
            prepare_col(m, col_feat[m])
            weigh_col(m, col_w[0, m])

        @pl.when((m < B) & (m > 0))
        def _():
            wait_slot(0, True, m, feat_ref, row_feat.at[m]).wait()
            wait_slot(1, True, m, init_ref, row_w.at[0, m]).wait()
            prepare_row(m, row_feat[m])
            weigh_row(m, row_w[0, m])

    units(True, arrive_first)
    sibling_unit(True)

    def partials(it):
        def of_row(acc):
            a = acc.T
            return -(a[0:1] + a[1:2] + a[2:3]), a[3:4]

        def of_col(acc):
            return acc[0:1] + acc[1:2] + acc[2:3], -acc[3:4]

        everything = jnp.zeros((1, n), f32)
        for d in range(1, B):
            y, t = of_row(row_acc[d])
            row_out[it, d] = jnp.concatenate([y, t], axis=0)
            everything += y
        for d in range(A):
            y, t = of_col(col_acc[d])
            col_out[it, d] = jnp.concatenate([y, t], axis=0)
            everything += y
        y0, t0 = of_row(row_acc[0])
        y1, t1 = of_col(col_acc[own])
        mine = jnp.concatenate([y0 + y1, t0 + t1], axis=0)
        return mine, everything + y0 + y1

    def send_partials(it):
        return exchange(
            2 + 2 * it,
            lambda d: row_out.at[it, d], lambda d: row_in.at[it, d],
            lambda d: col_out.at[it, d], lambda d: col_in.at[it, d], col_owner,
        )

    def receive(it, copies, mine):
        for (is_row, d), copy in copies.items():
            copy.wait()
            mine = mine + (row_in[it, d] if is_row else col_in[it, d])
        return mine

    def wide(x):
        return jnp.broadcast_to(x[:, 0:1], (1, n))

    step_rate = 1.0 / total
    mine, _ = partials(0)
    copies = send_partials(0)
    sum0 = wide(scal_finish(0))
    mine = receive(0, copies, mine)
    y, t = mine[0:1], mine[1:2]
    stay = 1.0 - step_rate * (0.5 * total + 0.5 * t)
    grown0 = step_rate * (0.5 * sum0 + 0.5 * y) + weights0 * stay
    grown[...] = grown0
    seconds = exchange(
        3, lambda d: grown, lambda d: row_w.at[1, d], lambda d: grown, lambda d: col_w.at[1, d], col_user
    )
    scal_start(1, lanes(grown0))

    row_acc[...] = jnp.zeros_like(row_acc)
    col_acc[...] = jnp.zeros_like(col_acc)
    weigh_row(0, grown0)
    weigh_col(own, grown0)

    def arrive_second(m):
        @pl.when(m < A)
        def _():
            wait_slot(3, False, m, grown, col_w.at[1, m]).wait()
            weigh_col(m, col_w[1, m])

        @pl.when((m < B) & (m > 0))
        def _():
            wait_slot(3, True, m, grown, row_w.at[1, m]).wait()
            weigh_row(m, row_w[1, m])

    units(False, arrive_second)
    sibling_unit(False)

    sum1 = wide(scal_finish(1))
    mine, everything = partials(1)
    copies = send_partials(1)
    base = step_rate * (0.5 * sum1) + grown0 * stay
    scal_start(2, lanes(base + (0.5 * step_rate) * everything))
    first_change = lanes(jnp.abs(grown0 / sum1 - weights0 / sum0))
    mine = receive(1, copies, mine)
    grown1 = base + (0.5 * step_rate) * mine[0:1]
    sum2 = wide(scal_finish(2))
    final = grown1 / sum2
    second_change = lanes(jnp.abs(final - grown0 / sum1))
    lane = lax.broadcasted_iota(jnp.int32, (1, 128), 1)
    scal_start(3, jnp.where(lane == 0, first_change, second_change))
    dist_ref[...] = total * final
    res_ref[...] = scal_finish(3)


def on_device(A, B, features, initial):
    feats, n = features.shape
    devices = 2 * A * B
    vmem = lambda *shape: pltpu.VMEM(shape, f32)
    dist, res = pl.pallas_call(
        functools.partial(kernel, A, B),
        out_shape=(jax.ShapeDtypeStruct((1, n), f32), jax.ShapeDtypeStruct((1, 128), f32)),
        in_specs=[pl.BlockSpec(memory_space=pltpu.VMEM)] * 2,
        out_specs=(pl.BlockSpec(memory_space=pltpu.VMEM),) * 2,
        scratch_shapes=[
            vmem(A, feats, n), vmem(B, feats, n), vmem(2, A, 1, n), vmem(2, B, 1, n),
            vmem(2, A, 2, n), vmem(2, B, 2, n), vmem(2, A, 2, n), vmem(2, B, 2, n), vmem(1, n),
            pltpu.VMEM((B, n, 4 * feats), bf16), pltpu.VMEM((A + 1, 4 * feats, n), bf16),
            pltpu.VMEM((B, 16, n), bf16), pltpu.VMEM((A + 1, n, 128), bf16),
            pltpu.VMEM((A * B + 1, n, n), bf16),
            vmem(B, n, 128), vmem(A + 1, 16, n), vmem(4, devices, 1, 128),
            pltpu.SemaphoreType.DMA((5, A + B)), pltpu.SemaphoreType.DMA((5, A + B)),
            pltpu.SemaphoreType.DMA((4, devices)), pltpu.SemaphoreType.DMA((4, devices)),
        ],
        compiler_params=pltpu.CompilerParams(
            collective_id=0, has_side_effects=True, vmem_limit_bytes=56 * 1024 * 1024
        ),
    )(features, initial.reshape(1, n))
    return dist.reshape(n), res[0, :2]


def solution(mesh):
    rows = mesh.shape["row"]
    B = 1
    while 4 * B * B <= rows:
        B *= 2
    A = rows // B
    placed = (P(None, ("row", "col")), P(("row", "col")))
    return jax.shard_map(
        functools.partial(on_device, A, B), mesh=mesh, in_specs=placed,
        out_specs=(P(("row", "col")), P()), check_vma=False,
    )
```

```python
import functools

import jax
import jax.numpy as jnp
from jax import lax
from jax.experimental import pallas as pl
from jax.experimental.pallas import tpu as pltpu
from jax.sharding import PartitionSpec as P

intensity = 0.25
ROW_TILE = 256
MESH_ID = pl.DeviceIdType.MESH
f32, bf16 = jnp.float32, jnp.bfloat16


def split3(x):
    hi = x.astype(bf16).astype(f32)
    mid = (x - hi).astype(bf16).astype(f32)
    return hi, mid, (x - hi - mid).astype(bf16).astype(f32)


def weight_rows(w, count):
    shape = (count, w.shape[1])
    hi, mid, low = (jnp.broadcast_to(v, shape) for v in split3(w))
    at = lax.broadcasted_iota(jnp.int32, shape, 0)
    tail = jnp.where(at == 3, 1.0, 0.0).astype(f32)
    return jnp.where(at == 0, hi, jnp.where(at == 1, mid, jnp.where(at == 2, low, tail)))


def kernel(
    A, B, feat_ref, init_ref, dist_ref, res_ref,
    col_feat, row_feat, col_w, row_w, col_in, row_in, col_out, row_out, grown,
    row_op, col_op, left, right, kept, row_acc, col_acc, scal,
    send_sem, recv_sem, scal_send, scal_recv,
):
    half = feat_ref.shape[0] // 2
    n = feat_ref.shape[1]
    devices = 2 * A * B
    total = n * devices
    row, core = lax.axis_index("row"), lax.axis_index("col")
    me = row * 2 + core
    p, q = lax.div(row, B), lax.rem(row, B)
    tile = min(ROW_TILE, n)
    own = A

    def later(x, y):
        return jnp.where(x > y, 1, 0)

    row_partner = [None] + [(p * B + (q ^ d), core) for d in range(1, B)]
    col_user = [(row, 1 - core)]
    col_owner = [(row, 1 - core)]
    for d in range(1, A):
        other = p ^ d
        col_user.append((other * B + q, core ^ later(p, other)))
        col_owner.append((other * B + q, core ^ later(other, p)))

    def exchange(round_id, row_src, row_dst, col_src, col_dst, col_to):
        copies = {}
        for d in range(max(A, B)):
            for is_row in (False, True):
                if d >= (B if is_row else A) or (is_row and d == 0):
                    continue
                slot = A + d if is_row else d
                copies[is_row, d] = pltpu.make_async_remote_copy(
                    src_ref=row_src(d) if is_row else col_src(d),
                    dst_ref=row_dst(d) if is_row else col_dst(d),
                    send_sem=send_sem.at[round_id, slot],
                    recv_sem=recv_sem.at[round_id, slot],
                    device_id=row_partner[d] if is_row else col_to[d],
                    device_id_type=MESH_ID,
                )
                copies[is_row, d].start()
        return copies

    def scal_copy(round_id, other, slot):
        return pltpu.make_async_remote_copy(
            src_ref=scal.at[round_id, me],
            dst_ref=scal.at[round_id, slot],
            send_sem=scal_send.at[round_id, other],
            recv_sem=scal_recv.at[round_id, slot],
            device_id=(lax.div(other, 2), lax.rem(other, 2)),
            device_id_type=MESH_ID,
        )

    def scal_start(round_id, value):
        scal[round_id, me] = value

        def one(k, carry):
            scal_copy(round_id, lax.rem(me + k, devices), me).start()
            return carry

        lax.fori_loop(1, devices, one, 0)

    def scal_finish(round_id):
        def one(k, carry):
            other = lax.rem(me + k, devices)
            scal_copy(round_id, other, other).wait()
            return carry

        lax.fori_loop(1, devices, one, 0)
        return jnp.sum(scal[round_id], axis=0)

    def lanes(x):
        return jnp.broadcast_to(jnp.sum(x, axis=1, keepdims=True), (1, 128))

    barrier = pltpu.get_barrier_semaphore()

    def greet(k, carry):
        other = lax.rem(me + k, devices)
        pl.semaphore_signal(
            barrier, inc=1, device_id=(lax.div(other, 2), lax.rem(other, 2)), device_id_type=MESH_ID
        )
        return carry

    lax.fori_loop(1, devices, greet, 0)
    pl.semaphore_wait(barrier, devices - 1)

    feats = exchange(
        0, lambda d: feat_ref, lambda d: row_feat.at[d], lambda d: feat_ref, lambda d: col_feat.at[d], col_user
    )
    starts = exchange(
        1, lambda d: init_ref, lambda d: row_w.at[0, d], lambda d: init_ref, lambda d: col_w.at[0, d], col_user
    )
    weights0 = init_ref[...]
    scal_start(0, lanes(weights0))

    row_acc[...] = jnp.zeros_like(row_acc)
    col_acc[...] = jnp.zeros_like(col_acc)

    def prepare_row(slot, f):
        g = jnp.concatenate([f[half:], -f[:half]], axis=0) * (0.5 * intensity)
        hi = g.astype(bf16).astype(f32)
        both = jnp.concatenate([hi, g - hi], axis=0)
        x = both.T.astype(bf16)
        row_op[slot] = jnp.concatenate([x, x], axis=1)

    def prepare_col(slot, f):
        hi = f.astype(bf16)
        low = (f - hi.astype(f32)).astype(bf16)
        col_op[slot] = jnp.concatenate([hi, hi, low, low], axis=0)

    def weigh_row(slot, w):
        left[slot] = weight_rows(w, 16).astype(bf16)

    def weigh_col(slot, w):
        right[slot] = w

    def unit(first, kept_slot, row_slot, col_slot, scale):
        down = jnp.zeros((16, n), f32)
        across_w = jnp.broadcast_to(right[col_slot], (8, n))
        for r in range(n // tile):
            at = pl.ds(r * tile, tile)
            if first:
                payoff = jnp.dot(row_op[row_slot, at], col_op[col_slot], preferred_element_type=f32)
                wide_t = jnp.tanh(payoff)
                t = wide_t.astype(bf16)
                kept[kept_slot, at] = t
            else:
                t = kept[kept_slot, at]
                wide_t = t.astype(f32)
            weighed = jnp.zeros((tile, 128), f32)
            plain = jnp.zeros((tile, 128), f32)
            for k in range(n // 128):
                part = wide_t[:, k * 128:(k + 1) * 128]
                by = across_w[:, k * 128:(k + 1) * 128]
                weighed += (part.reshape(tile // 8, 8, 128) * by[None]).reshape(tile, 128)
                if first:
                    plain += part
            row_acc[0, row_slot, at] += weighed if scale is None else scale * weighed
            if first:
                row_acc[1, row_slot, at] += plain if scale is None else scale * plain
            down += jnp.dot(left[row_slot, :, r * tile:(r + 1) * tile], t, preferred_element_type=f32)
        col_acc[col_slot] += down if scale is None else scale * down

    def units(first, arrive):
        def near(j, carry):
            @pl.when(j == 1)
            def _():
                arrive(0)

            unit(first, jnp.where(j == 0, 0, A * B), 0, jnp.where(j == 0, own, 0), 0.5)
            return carry

        lax.fori_loop(0, 2, near, 0)

        def shell(m, carry):
            arrive(m)

            def one(j, carry):
                dq = jnp.where(j <= m, m, j - m - 1)
                dp = jnp.where(j <= m, j, m)
                own_or_sibling = jnp.where((q ^ dq) > q, 0, own)
                col_slot = jnp.where(dp == 0, own_or_sibling, dp)

                def run():
                    unit(first, dq * A + dp, dq, col_slot, None)

                if A == B:
                    run()
                else:
                    pl.when((dq < B) & (dp < A))(run)
                return carry

            return lax.fori_loop(0, 2 * m + 1, one, carry)

        lax.fori_loop(1, max(A, B), shell, 0)

    def wait_slot(copies_sem_round, is_row, d, src, dst):
        slot = A + d if is_row else d
        return pltpu.make_async_remote_copy(
            src_ref=src, dst_ref=dst, send_sem=send_sem.at[copies_sem_round, slot],
            recv_sem=recv_sem.at[copies_sem_round, slot], device_id=(row, 1 - core), device_id_type=MESH_ID,
        )

    prepare_row(0, feat_ref[...])
    prepare_col(own, feat_ref[...])
    weigh_row(0, weights0)
    weigh_col(own, weights0)

    def arrive_first(m):
        @pl.when(m < A)
        def _():
            wait_slot(0, False, m, feat_ref, col_feat.at[m]).wait()
            wait_slot(1, False, m, init_ref, col_w.at[0, m]).wait()
            prepare_col(m, col_feat[m])
            weigh_col(m, col_w[0, m])

        @pl.when((m < B) & (m > 0))
        def _():
            wait_slot(0, True, m, feat_ref, row_feat.at[m]).wait()
            wait_slot(1, True, m, init_ref, row_w.at[0, m]).wait()
            prepare_row(m, row_feat[m])
            weigh_row(m, row_w[0, m])

    units(True, arrive_first)

    def partials(it):
        def of_row(d):
            y = jnp.sum(row_acc[0, d].T, axis=0, keepdims=True)
            t = jnp.sum(row_acc[1, d].T, axis=0, keepdims=True) if it == 0 else jnp.zeros((1, n), f32)
            return -y, t

        def of_col(acc):
            return acc[0:1] + acc[1:2] + acc[2:3], -acc[3:4]

        everything = jnp.zeros((1, n), f32)
        for d in range(1, B):
            y, t = of_row(d)
            row_out[it, d] = jnp.concatenate([y, t], axis=0)
            everything += y
        for d in range(A):
            y, t = of_col(col_acc[d])
            col_out[it, d] = jnp.concatenate([y, t], axis=0)
            everything += y
        y0, t0 = of_row(0)
        y1, t1 = of_col(col_acc[own])
        mine = jnp.concatenate([y0 + y1, t0 + t1], axis=0)
        return mine, everything + y0 + y1

    def send_partials(it):
        return exchange(
            2 + 2 * it,
            lambda d: row_out.at[it, d], lambda d: row_in.at[it, d],
            lambda d: col_out.at[it, d], lambda d: col_in.at[it, d], col_owner,
        )

    def receive(it, copies, mine):
        for (is_row, d), copy in copies.items():
            copy.wait()
            mine = mine + (row_in[it, d] if is_row else col_in[it, d])
        return mine

    def wide(x):
        return jnp.broadcast_to(x[:, 0:1], (1, n))

    step_rate = 1.0 / total
    mine, _ = partials(0)
    copies = send_partials(0)
    sum0 = wide(scal_finish(0))
    mine = receive(0, copies, mine)
    y, t = mine[0:1], mine[1:2]
    stay = 1.0 - step_rate * (0.5 * total + 0.5 * t)
    grown0 = step_rate * (0.5 * sum0 + 0.5 * y) + weights0 * stay
    grown[...] = grown0
    seconds = exchange(
        3, lambda d: grown, lambda d: row_w.at[1, d], lambda d: grown, lambda d: col_w.at[1, d], col_user
    )
    scal_start(1, lanes(grown0))

    row_acc[...] = jnp.zeros_like(row_acc)
    col_acc[...] = jnp.zeros_like(col_acc)
    weigh_row(0, grown0)
    weigh_col(own, grown0)

    def arrive_second(m):
        @pl.when(m < A)
        def _():
            wait_slot(3, False, m, grown, col_w.at[1, m]).wait()
            weigh_col(m, col_w[1, m])

        @pl.when((m < B) & (m > 0))
        def _():
            wait_slot(3, True, m, grown, row_w.at[1, m]).wait()
            weigh_row(m, row_w[1, m])

    units(False, arrive_second)

    sum1 = wide(scal_finish(1))
    mine, everything = partials(1)
    copies = send_partials(1)
    base = step_rate * (0.5 * sum1) + grown0 * stay
    scal_start(2, lanes(base + (0.5 * step_rate) * everything))
    first_change = lanes(jnp.abs(grown0 / sum1 - weights0 / sum0))
    mine = receive(1, copies, mine)
    grown1 = base + (0.5 * step_rate) * mine[0:1]
    sum2 = wide(scal_finish(2))
    final = grown1 / sum2
    second_change = lanes(jnp.abs(final - grown0 / sum1))
    lane = lax.broadcasted_iota(jnp.int32, (1, 128), 1)
    scal_start(3, jnp.where(lane == 0, first_change, second_change))
    dist_ref[...] = (total * final).reshape(n)
    both = scal_finish(3)
    res_ref[0] = jnp.sum(jnp.where(lane == 0, both, 0.0))
    res_ref[1] = jnp.sum(jnp.where(lane == 1, both, 0.0))


def on_device(A, B, features, initial):
    feats, n = features.shape
    devices = 2 * A * B
    vmem = lambda *shape: pltpu.VMEM(shape, f32)
    dist, res = pl.pallas_call(
        functools.partial(kernel, A, B),
        out_shape=(jax.ShapeDtypeStruct((n,), f32), jax.ShapeDtypeStruct((2,), f32)),
        in_specs=[pl.BlockSpec(memory_space=pltpu.VMEM)] * 2,
        out_specs=(pl.BlockSpec(memory_space=pltpu.VMEM), pl.BlockSpec(memory_space=pltpu.SMEM)),
        scratch_shapes=[
            vmem(A, feats, n), vmem(B, feats, n), vmem(2, A, 1, n), vmem(2, B, 1, n),
            vmem(2, A, 2, n), vmem(2, B, 2, n), vmem(2, A, 2, n), vmem(2, B, 2, n), vmem(1, n),
            pltpu.VMEM((B, n, 4 * feats), bf16), pltpu.VMEM((A + 1, 4 * feats, n), bf16),
            pltpu.VMEM((B, 16, n), bf16), vmem(A + 1, 1, n),
            pltpu.VMEM((A * B + 1, n, n), bf16),
            vmem(2, B, n, 128), vmem(A + 1, 16, n), vmem(4, devices, 1, 128),
            pltpu.SemaphoreType.DMA((5, A + B)), pltpu.SemaphoreType.DMA((5, A + B)),
            pltpu.SemaphoreType.DMA((4, devices)), pltpu.SemaphoreType.DMA((4, devices)),
        ],
        compiler_params=pltpu.CompilerParams(
            collective_id=0, has_side_effects=True, vmem_limit_bytes=56 * 1024 * 1024
        ),
    )(features, initial.reshape(1, n))
    return dist, res


def solution(mesh):
    rows = mesh.shape["row"]
    B = 1
    while 4 * B * B <= rows:
        B *= 2
    A = rows // B
    placed = (P(None, ("row", "col")), P(("row", "col")))
    return jax.shard_map(
        functools.partial(on_device, A, B), mesh=mesh, in_specs=placed,
        out_specs=(P(("row", "col")), P()), check_vma=False,
    )
```

```python
import functools

import jax
import jax.numpy as jnp
from jax import lax
from jax.experimental import pallas as pl
from jax.experimental.pallas import tpu as pltpu
from jax.sharding import PartitionSpec as P

intensity = 0.25
ROW_TILE = 256
MESH_ID = pl.DeviceIdType.MESH
f32, bf16 = jnp.float32, jnp.bfloat16


def split3(x):
    hi = x.astype(bf16).astype(f32)
    mid = (x - hi).astype(bf16).astype(f32)
    return hi, mid, (x - hi - mid).astype(bf16).astype(f32)


def weight_rows(w, count):
    shape = (count, w.shape[1])
    hi, mid, low = (jnp.broadcast_to(v, shape) for v in split3(w))
    at = lax.broadcasted_iota(jnp.int32, shape, 0)
    tail = jnp.where(at == 3, 1.0, 0.0).astype(f32)
    return jnp.where(at == 0, hi, jnp.where(at == 1, mid, jnp.where(at == 2, low, tail)))


def kernel(
    A, B, feat_ref, init_ref, dist_ref, res_ref,
    col_feat, row_feat, col_w, row_w, col_in, row_in, col_out, row_out, grown,
    row_op, col_op, left, right, kept, row_acc, col_acc, scal,
    send_sem, recv_sem, scal_send, scal_recv,
):
    half = feat_ref.shape[0] // 2
    n = feat_ref.shape[1]
    devices = 2 * A * B
    total = n * devices
    row, core = lax.axis_index("row"), lax.axis_index("col")
    me = row * 2 + core
    p, q = lax.div(row, B), lax.rem(row, B)
    tile = min(ROW_TILE, n)
    own = A

    def later(x, y):
        return jnp.where(x > y, 1, 0)

    row_partner = [None] + [(p * B + (q ^ d), core) for d in range(1, B)]
    others = [p] + [lax.rem(p + d, A) for d in range(1, A)]
    col_user = [(row, 1 - core)] + [(o * B + q, core ^ later(p, o)) for o in others[1:]]
    col_owner = [(row, 1 - core)] + [(o * B + q, core ^ later(o, p)) for o in others[1:]]

    def copy_to(round_id, src, dst, send_slot, recv_slot, device):
        return pltpu.make_async_remote_copy(
            src_ref=src, dst_ref=dst, send_sem=send_sem.at[round_id, send_slot],
            recv_sem=recv_sem.at[round_id, recv_slot], device_id=device, device_id_type=MESH_ID,
        )

    def row_copies(round_id, src, dst):
        return [
            copy_to(round_id, src(d), dst.at[d], A + d, A + d, row_partner[d]) for d in range(1, B)
        ]

    def col_copies(round_id, src, dst, to):
        return [copy_to(round_id, src(d), dst.at[p], d, p, to[d]) for d in range(A)]

    def landed(round_id, dst, slot, sem_slot):
        copy_to(round_id, dst.at[slot], dst.at[slot], sem_slot, sem_slot, (row, 1 - core)).wait_recv()

    can_up, can_down = p < A - 1, p > 0
    up, down_at = ((p + 1) * B + q, core), ((p - 1) * B + q, core)
    own_up = copy_to(0, feat_ref, col_feat.at[p], A + B, p, up)
    own_down = copy_to(0, feat_ref, col_feat.at[p], A + B + 1, p, ((p - 1) * B + q, 1 - core))
    to_sibling = copy_to(0, feat_ref, col_feat.at[p], p, p, (row, 1 - core))

    def pass_on(o, act):
        @pl.when((o < p) & can_up)
        def _():
            act(copy_to(0, col_feat.at[o], col_feat.at[o], o, o, up))

        @pl.when((o > p) & can_down)
        def _():
            act(copy_to(0, col_feat.at[o], col_feat.at[o], o, o, down_at))

    def at_distance(m):
        above = A - 1 - p
        near = jnp.minimum(p, above)
        step = lax.div(m + 1, 2)
        mixed = jnp.where(lax.rem(m, 2) == 1, p - step, p + step)
        rest = jnp.where(above > p, p + m - near, p - m + near)
        return jnp.where(m <= 2 * near, mixed, rest)

    def scal_copy(round_id, other, slot):
        return pltpu.make_async_remote_copy(
            src_ref=scal.at[round_id, me],
            dst_ref=scal.at[round_id, slot],
            send_sem=scal_send.at[round_id, other],
            recv_sem=scal_recv.at[round_id, slot],
            device_id=(lax.div(other, 2), lax.rem(other, 2)),
            device_id_type=MESH_ID,
        )

    def scal_start(round_id, value):
        scal[round_id, me] = value

        def one(k, carry):
            scal_copy(round_id, lax.rem(me + k, devices), me).start()
            return carry

        lax.fori_loop(1, devices, one, 0)

    def scal_finish(round_id):
        def one(k, carry):
            other = lax.rem(me + k, devices)
            scal_copy(round_id, other, other).wait()
            return carry

        lax.fori_loop(1, devices, one, 0)
        return jnp.sum(scal[round_id], axis=0)

    def lanes(x):
        return jnp.broadcast_to(jnp.sum(x, axis=1, keepdims=True), (1, 128))

    barrier = pltpu.get_barrier_semaphore()

    def greet(k, carry):
        other = lax.rem(me + k, devices)
        pl.semaphore_signal(
            barrier, inc=1, device_id=(lax.div(other, 2), lax.rem(other, 2)), device_id_type=MESH_ID
        )
        return carry

    lax.fori_loop(1, devices, greet, 0)
    pl.semaphore_wait(barrier, devices - 1)

    to_sibling.start()

    @pl.when(can_up)
    def _():
        own_up.start()

    @pl.when(can_down)
    def _():
        own_down.start()

    feat_rows = row_copies(0, lambda d: feat_ref, row_feat)
    start_rows = row_copies(1, lambda d: init_ref, row_w.at[0])
    start_cols = col_copies(1, lambda d: init_ref, col_w.at[0], col_user)
    for copy in feat_rows + start_rows + start_cols:
        copy.start()
    weights0 = init_ref[...]
    scal_start(0, lanes(weights0))

    row_acc[...] = jnp.zeros_like(row_acc)
    col_acc[...] = jnp.zeros_like(col_acc)

    def prepare_row(slot, f):
        g = jnp.concatenate([f[half:], -f[:half]], axis=0) * (0.5 * intensity)
        hi = g.astype(bf16).astype(f32)
        both = jnp.concatenate([hi, g - hi], axis=0)
        x = both.T.astype(bf16)
        row_op[slot] = jnp.concatenate([x, x], axis=1)

    def prepare_col(slot, f):
        hi = f.astype(bf16)
        low = (f - hi.astype(f32)).astype(bf16)
        col_op[slot] = jnp.concatenate([hi, hi, low, low], axis=0)

    def weigh_row(slot, w):
        left[slot] = weight_rows(w, 16).astype(bf16)

    def weigh_col(slot, w):
        right[slot] = w

    def unit(first, kept_slot, row_slot, col_slot, scale):
        down = jnp.zeros((16, n), f32)
        across_w = jnp.broadcast_to(right[col_slot], (8, n))
        for r in range(n // tile):
            at = pl.ds(r * tile, tile)
            if first:
                payoff = jnp.dot(row_op[row_slot, at], col_op[col_slot], preferred_element_type=f32)
                wide_t = jnp.tanh(payoff)
                t = wide_t.astype(bf16)
                kept[kept_slot, at] = t
            else:
                t = kept[kept_slot, at]
                wide_t = t.astype(f32)
            weighed = jnp.zeros((tile, 128), f32)
            plain = jnp.zeros((tile, 128), f32)
            for k in range(n // 128):
                part = wide_t[:, k * 128:(k + 1) * 128]
                by = across_w[:, k * 128:(k + 1) * 128]
                weighed += (part.reshape(tile // 8, 8, 128) * by[None]).reshape(tile, 128)
                if first:
                    plain += part
            row_acc[0, row_slot, at] += weighed if scale is None else scale * weighed
            if first:
                row_acc[1, row_slot, at] += plain if scale is None else scale * plain
            down += jnp.dot(left[row_slot, :, r * tile:(r + 1) * tile], t, preferred_element_type=f32)
        col_acc[col_slot] += down if scale is None else scale * down

    def units(first, land, arrive):
        def near(j, carry):
            @pl.when(j == 1)
            def _():
                land(0)
                arrive(0)

            unit(first, jnp.where(j == 0, 0, A * B), 0, jnp.where(j == 0, own, p), 0.5)
            return carry

        lax.fori_loop(0, 2, near, 0)

        def shell(m, carry):
            @pl.when((m == 1) | jnp.logical_not(can_up & can_down))
            def _():
                land(m)

            arrive(m)

            def one(j, carry):
                dq = jnp.where(j <= m, m, j - m - 1)
                dp = jnp.where(j <= m, j, m)
                own_or_sibling = jnp.where((q ^ dq) > q, p, own)
                col_slot = jnp.where(dp == 0, own_or_sibling, at_distance(jnp.maximum(dp, 1)))

                @pl.when((j == m) & (m < max(A, B) - 1) & can_up & can_down)
                def _():
                    land(m + 1)

                def run():
                    unit(first, dq * A + dp, dq, col_slot, None)

                if A == B:
                    run()
                else:
                    pl.when((dq < B) & (dp < A))(run)
                return carry

            return lax.fori_loop(0, 2 * m + 1, one, carry)

        lax.fori_loop(1, max(A, B), shell, 0)

    prepare_row(0, feat_ref[...])
    prepare_col(own, feat_ref[...])
    weigh_row(0, weights0)
    weigh_col(own, weights0)

    def place(m):
        return jnp.where(m == 0, p, at_distance(jnp.maximum(m, 1)))

    def land_first(m):
        @pl.when(m < A)
        def _():
            o = place(m)
            landed(0, col_feat, o, o)
            pass_on(o, lambda copy: copy.start())

    def arrive_first(m):
        @pl.when(m < A)
        def _():
            o = place(m)
            landed(1, col_w.at[0], o, o)
            prepare_col(o, col_feat[o])
            weigh_col(o, col_w[0, o])

        @pl.when((m < B) & (m > 0))
        def _():
            landed(0, row_feat, m, A + m)
            landed(1, row_w.at[0], m, A + m)
            prepare_row(m, row_feat[m])
            weigh_row(m, row_w[0, m])

    units(True, land_first, arrive_first)

    def partials(it):
        def of_row(d):
            y = jnp.sum(row_acc[0, d].T, axis=0, keepdims=True)
            t = jnp.sum(row_acc[1, d].T, axis=0, keepdims=True) if it == 0 else jnp.zeros((1, n), f32)
            return -y, t

        def of_col(acc):
            return acc[0:1] + acc[1:2] + acc[2:3], -acc[3:4]

        everything = jnp.zeros((1, n), f32)
        for d in range(1, B):
            y, t = of_row(d)
            row_out[it, d] = jnp.concatenate([y, t], axis=0)
            everything += y
        for d in range(A):
            y, t = of_col(col_acc[others[d]])
            col_out[it, d] = jnp.concatenate([y, t], axis=0)
            everything += y
        y0, t0 = of_row(0)
        y1, t1 = of_col(col_acc[own])
        mine = jnp.concatenate([y0 + y1, t0 + t1], axis=0)
        return mine, everything + y0 + y1

    def send_partials(it):
        copies = row_copies(2 + 2 * it, lambda d: row_out.at[it, d], row_in.at[it])
        copies += col_copies(2 + 2 * it, lambda d: col_out.at[it, d], col_in.at[it], col_owner)
        for copy in copies:
            copy.start()
        return copies

    def receive(it, mine):
        for d in range(1, B):
            landed(2 + 2 * it, row_in.at[it], d, A + d)
            mine = mine + row_in[it, d]
        for d in range(A):
            landed(2 + 2 * it, col_in.at[it], d, d)
            mine = mine + col_in[it, d]
        return mine

    def wide(x):
        return jnp.broadcast_to(x[:, 0:1], (1, n))

    step_rate = 1.0 / total
    mine, _ = partials(0)
    sent = send_partials(0)
    sum0 = wide(scal_finish(0))
    mine = receive(0, mine)
    y, t = mine[0:1], mine[1:2]
    stay = 1.0 - step_rate * (0.5 * total + 0.5 * t)
    grown0 = step_rate * (0.5 * sum0 + 0.5 * y) + weights0 * stay
    grown[...] = grown0
    seconds = row_copies(3, lambda d: grown, row_w.at[1]) + col_copies(3, lambda d: grown, col_w.at[1], col_user)
    for copy in seconds:
        copy.start()
    scal_start(1, lanes(grown0))

    row_acc[...] = jnp.zeros_like(row_acc)
    col_acc[...] = jnp.zeros_like(col_acc)
    weigh_row(0, grown0)
    weigh_col(own, grown0)

    def arrive_second(m):
        @pl.when(m < A)
        def _():
            o = place(m)
            landed(3, col_w.at[1], o, o)
            weigh_col(o, col_w[1, o])

        @pl.when((m < B) & (m > 0))
        def _():
            landed(3, row_w.at[1], m, A + m)
            weigh_row(m, row_w[1, m])

    units(False, lambda m: None, arrive_second)

    sum1 = wide(scal_finish(1))
    mine, everything = partials(1)
    sent += send_partials(1)
    base = step_rate * (0.5 * sum1) + grown0 * stay
    scal_start(2, lanes(base + (0.5 * step_rate) * everything))
    first_change = lanes(jnp.abs(grown0 / sum1 - weights0 / sum0))
    mine = receive(1, mine)
    grown1 = base + (0.5 * step_rate) * mine[0:1]
    sum2 = wide(scal_finish(2))
    final = grown1 / sum2
    second_change = lanes(jnp.abs(final - grown0 / sum1))
    lane = lax.broadcasted_iota(jnp.int32, (1, 128), 1)
    scal_start(3, jnp.where(lane == 0, first_change, second_change))
    dist_ref[...] = (total * final).reshape(n)
    both = scal_finish(3)
    res_ref[0] = jnp.sum(jnp.where(lane == 0, both, 0.0))
    res_ref[1] = jnp.sum(jnp.where(lane == 1, both, 0.0))

    for copy in feat_rows + start_rows + start_cols + seconds + sent + [to_sibling]:
        copy.wait_send()

    @pl.when(can_up)
    def _():
        own_up.wait_send()

    @pl.when(can_down)
    def _():
        own_down.wait_send()

    for o in others[1:]:
        pass_on(o, lambda copy: copy.wait_send())


def on_device(A, B, features, initial):
    feats, n = features.shape
    devices = 2 * A * B
    vmem = lambda *shape: pltpu.VMEM(shape, f32)
    dist, res = pl.pallas_call(
        functools.partial(kernel, A, B),
        out_shape=(jax.ShapeDtypeStruct((n,), f32), jax.ShapeDtypeStruct((2,), f32)),
        in_specs=[pl.BlockSpec(memory_space=pltpu.VMEM)] * 2,
        out_specs=(pl.BlockSpec(memory_space=pltpu.VMEM), pl.BlockSpec(memory_space=pltpu.SMEM)),
        scratch_shapes=[
            vmem(A, feats, n), vmem(B, feats, n), vmem(2, A, 1, n), vmem(2, B, 1, n),
            vmem(2, A, 2, n), vmem(2, B, 2, n), vmem(2, A, 2, n), vmem(2, B, 2, n), vmem(1, n),
            pltpu.VMEM((B, n, 4 * feats), bf16), pltpu.VMEM((A + 1, 4 * feats, n), bf16),
            pltpu.VMEM((B, 16, n), bf16), vmem(A + 1, 1, n),
            pltpu.VMEM((A * B + 1, n, n), bf16),
            vmem(2, B, n, 128), vmem(A + 1, 16, n), vmem(4, devices, 1, 128),
            pltpu.SemaphoreType.DMA((5, A + B + 2)), pltpu.SemaphoreType.DMA((5, A + B)),
            pltpu.SemaphoreType.DMA((4, devices)), pltpu.SemaphoreType.DMA((4, devices)),
        ],
        compiler_params=pltpu.CompilerParams(
            collective_id=0, has_side_effects=True, vmem_limit_bytes=56 * 1024 * 1024
        ),
    )(features, initial.reshape(1, n))
    return dist, res


def solution(mesh):
    rows = mesh.shape["row"]
    B = 1
    while 4 * B * B <= rows:
        B *= 2
    A = rows // B
    placed = (P(None, ("row", "col")), P(("row", "col")))
    return jax.shard_map(
        functools.partial(on_device, A, B), mesh=mesh, in_specs=placed,
        out_specs=(P(("row", "col")), P()), check_vma=False,
    )
```

```python
import functools

import jax
import jax.numpy as jnp
from jax import lax
from jax.experimental import pallas as pl
from jax.experimental.pallas import tpu as pltpu
from jax.sharding import PartitionSpec as P

intensity = 0.25
ROW_TILE = 256
MESH_ID = pl.DeviceIdType.MESH
f32, bf16 = jnp.float32, jnp.bfloat16


def split3(x):
    hi = x.astype(bf16).astype(f32)
    mid = (x - hi).astype(bf16).astype(f32)
    return hi, mid, (x - hi - mid).astype(bf16).astype(f32)


def weight_rows(w, count):
    shape = (count, w.shape[1])
    hi, mid, low = (jnp.broadcast_to(v, shape) for v in split3(w))
    at = lax.broadcasted_iota(jnp.int32, shape, 0)
    tail = jnp.where(at == 3, 1.0, 0.0).astype(f32)
    return jnp.where(at == 0, hi, jnp.where(at == 1, mid, jnp.where(at == 2, low, tail)))


def kernel(
    A, B, feat_ref, init_ref, dist_ref, res_ref,
    col_feat, row_feat, col_w, row_w, col_in, row_in, col_out, row_out, grown,
    row_op, col_op, left, right, kept, row_acc, col_acc, scal,
    send_sem, recv_sem, scal_send, scal_recv,
):
    half = feat_ref.shape[0] // 2
    n = feat_ref.shape[1]
    devices = 2 * A * B
    total = n * devices
    row, core = lax.axis_index("row"), lax.axis_index("col")
    me = row * 2 + core
    p, q = lax.div(row, B), lax.rem(row, B)
    tile = min(ROW_TILE, n)
    own = A

    def later(x, y):
        return jnp.where(x > y, 1, 0)

    row_partner = [None] + [(p * B + (q ^ d), core) for d in range(1, B)]
    others = [p] + [lax.rem(p + d, A) for d in range(1, A)]
    col_user = [(row, 1 - core)] + [(o * B + q, core ^ later(p, o)) for o in others[1:]]
    col_owner = [(row, 1 - core)] + [(o * B + q, core ^ later(o, p)) for o in others[1:]]

    def copy_to(round_id, src, dst, send_slot, recv_slot, device):
        return pltpu.make_async_remote_copy(
            src_ref=src, dst_ref=dst, send_sem=send_sem.at[round_id, send_slot],
            recv_sem=recv_sem.at[round_id, recv_slot], device_id=device, device_id_type=MESH_ID,
        )

    def row_copies(round_id, src, dst):
        return [
            copy_to(round_id, src(d), dst.at[d], A + d, A + d, row_partner[d]) for d in range(1, B)
        ]

    def col_copies(round_id, src, dst, to):
        return [copy_to(round_id, src(d), dst.at[p], d, p, to[d]) for d in range(A)]

    def landed(round_id, dst, slot, sem_slot):
        copy_to(round_id, dst.at[slot], dst.at[slot], sem_slot, sem_slot, (row, 1 - core)).wait_recv()

    can_up, can_down = p < A - 1, p > 0
    up, down_at = ((p + 1) * B + q, core), ((p - 1) * B + q, core)
    own_up = copy_to(0, feat_ref, col_feat.at[p], A + B, p, up)
    own_down = copy_to(0, feat_ref, col_feat.at[p], A + B + 1, p, ((p - 1) * B + q, 1 - core))
    to_sibling = copy_to(0, feat_ref, col_feat.at[p], p, p, (row, 1 - core))

    def pass_on(o, act):
        @pl.when((o < p) & can_up)
        def _():
            act(copy_to(0, col_feat.at[o], col_feat.at[o], o, o, up))

        @pl.when((o > p) & can_down)
        def _():
            act(copy_to(0, col_feat.at[o], col_feat.at[o], o, o, down_at))

    def at_distance(m):
        above = A - 1 - p
        near = jnp.minimum(p, above)
        step = lax.div(m + 1, 2)
        mixed = jnp.where(lax.rem(m, 2) == 1, p - step, p + step)
        rest = jnp.where(above > p, p + m - near, p - m + near)
        return jnp.where(m <= 2 * near, mixed, rest)

    def all_others(act):
        if devices <= 64:
            for k in range(1, devices):
                act((row ^ (k // 2), core ^ (k % 2)))
        else:
            def one(k, carry):
                act((row ^ lax.div(k, 2), core ^ lax.rem(k, 2)))
                return carry

            lax.fori_loop(1, devices, one, 0)

    def scal_start(round_id, value):
        scal[round_id, me] = value
        all_others(lambda device: pltpu.make_async_remote_copy(
            src_ref=scal.at[round_id, me], dst_ref=scal.at[round_id, me], send_sem=scal_send.at[round_id],
            recv_sem=scal_recv.at[round_id], device_id=device, device_id_type=MESH_ID,
        ).start())

    def scal_finish(round_id):
        every = scal.at[round_id, pl.ds(0, devices - 1)]
        copy = pltpu.make_async_remote_copy(
            src_ref=every, dst_ref=every, send_sem=scal_send.at[round_id],
            recv_sem=scal_recv.at[round_id], device_id=(row, 1 - core), device_id_type=MESH_ID,
        )
        copy.wait_recv()
        copy.wait_send()
        return jnp.sum(scal[round_id], axis=0)

    def lanes(x):
        return jnp.broadcast_to(jnp.sum(x, axis=1, keepdims=True), (1, 128))

    def prepare_row(slot, f):
        g = jnp.concatenate([f[half:], -f[:half]], axis=0) * (0.5 * intensity)
        hi = g.astype(bf16).astype(f32)
        both = jnp.concatenate([hi, g - hi], axis=0)
        x = both.T.astype(bf16)
        row_op[slot] = jnp.concatenate([x, x], axis=1)

    def prepare_col(slot, f):
        hi = f.astype(bf16)
        low = (f - hi.astype(f32)).astype(bf16)
        col_op[slot] = jnp.concatenate([hi, hi, low, low], axis=0)

    def weigh_row(slot, w):
        left[slot] = weight_rows(w, 16).astype(bf16)

    def weigh_col(slot, w):
        right[slot] = w

    barrier = pltpu.get_barrier_semaphore()

    all_others(lambda device: pl.semaphore_signal(
        barrier, inc=1, device_id=device, device_id_type=MESH_ID
    ))

    weights0 = init_ref[...]
    row_acc[...] = jnp.zeros_like(row_acc)
    col_acc[...] = jnp.zeros_like(col_acc)
    prepare_row(0, feat_ref[...])
    prepare_col(own, feat_ref[...])
    weigh_row(0, weights0)
    weigh_col(own, weights0)
    pl.semaphore_wait(barrier, devices - 1)

    to_sibling.start()

    @pl.when(can_up)
    def _():
        own_up.start()

    @pl.when(can_down)
    def _():
        own_down.start()

    feat_rows = row_copies(0, lambda d: feat_ref, row_feat)
    start_rows = row_copies(1, lambda d: init_ref, row_w.at[0])
    start_cols = col_copies(1, lambda d: init_ref, col_w.at[0], col_user)
    for copy in feat_rows + start_rows + start_cols:
        copy.start()
    def unit(first, kept_slot, row_slot, col_slot, scale):
        down = jnp.zeros((16, n), f32)
        across_w = jnp.broadcast_to(right[col_slot], (8, n))
        for r in range(n // tile):
            at = pl.ds(r * tile, tile)
            if first:
                payoff = jnp.dot(row_op[row_slot, at], col_op[col_slot], preferred_element_type=f32)
                wide_t = jnp.tanh(payoff)
                t = wide_t.astype(bf16)
                kept[kept_slot, at] = t
            else:
                t = kept[kept_slot, at]
                wide_t = t.astype(f32)
            weighed = jnp.zeros((tile, 128), f32)
            plain = jnp.zeros((tile, 128), f32)
            for k in range(n // 128):
                part = wide_t[:, k * 128:(k + 1) * 128]
                by = across_w[:, k * 128:(k + 1) * 128]
                weighed += (part.reshape(tile // 8, 8, 128) * by[None]).reshape(tile, 128)
                if first:
                    plain += part
            row_acc[0, row_slot, at] += weighed if scale is None else scale * weighed
            if first:
                row_acc[1, row_slot, at] += plain if scale is None else scale * plain
            down += jnp.dot(left[row_slot, :, r * tile:(r + 1) * tile], t, preferred_element_type=f32)
        col_acc[col_slot] += down if scale is None else scale * down

    def units(first, land, arrive, between):
        def near(j, carry):
            @pl.when(j == 1)
            def _():
                land(0)
                arrive(0)

            unit(first, jnp.where(j == 0, 0, A * B), 0, jnp.where(j == 0, own, p), 0.5)
            return carry

        lax.fori_loop(0, 2, near, 0)
        between()

        def shell(m, carry):
            @pl.when((m == 1) | jnp.logical_not(can_up & can_down))
            def _():
                land(m)

            arrive(m)

            def one(j, carry):
                dq = jnp.where(j <= m, m, j - m - 1)
                dp = jnp.where(j <= m, j, m)
                own_or_sibling = jnp.where((q ^ dq) > q, p, own)
                col_slot = jnp.where(dp == 0, own_or_sibling, at_distance(jnp.maximum(dp, 1)))

                @pl.when((j == m) & (m < max(A, B) - 1) & can_up & can_down)
                def _():
                    land(m + 1)

                def run():
                    unit(first, dq * A + dp, dq, col_slot, None)

                if A == B:
                    run()
                else:
                    pl.when((dq < B) & (dp < A))(run)
                return carry

            return lax.fori_loop(0, 2 * m + 1, one, carry)

        lax.fori_loop(1, max(A, B), shell, 0)


    def place(m):
        return jnp.where(m == 0, p, at_distance(jnp.maximum(m, 1)))

    def land_first(m):
        @pl.when(m < A)
        def _():
            o = place(m)
            landed(0, col_feat, o, o)
            pass_on(o, lambda copy: copy.start())

    def arrive_first(m):
        @pl.when(m < A)
        def _():
            o = place(m)
            landed(1, col_w.at[0], o, o)
            prepare_col(o, col_feat[o])
            weigh_col(o, col_w[0, o])

        @pl.when((m < B) & (m > 0))
        def _():
            landed(0, row_feat, m, A + m)
            landed(1, row_w.at[0], m, A + m)
            prepare_row(m, row_feat[m])
            weigh_row(m, row_w[0, m])

    units(True, land_first, arrive_first, lambda: scal_start(0, lanes(weights0)))

    def partials(it):
        def of_row(d):
            y = jnp.sum(row_acc[0, d].T, axis=0, keepdims=True)
            t = jnp.sum(row_acc[1, d].T, axis=0, keepdims=True) if it == 0 else jnp.zeros((1, n), f32)
            return -y, t

        def of_col(acc):
            return acc[0:1] + acc[1:2] + acc[2:3], -acc[3:4]

        everything = jnp.zeros((1, n), f32)
        for d in range(1, B):
            y, t = of_row(d)
            row_out[it, d] = jnp.concatenate([y, t], axis=0)
            everything += y
        for d in range(A):
            y, t = of_col(col_acc[others[d]])
            col_out[it, d] = jnp.concatenate([y, t], axis=0)
            everything += y
        y0, t0 = of_row(0)
        y1, t1 = of_col(col_acc[own])
        mine = jnp.concatenate([y0 + y1, t0 + t1], axis=0)
        return mine, everything + y0 + y1

    def send_partials(it):
        copies = row_copies(2 + 2 * it, lambda d: row_out.at[it, d], row_in.at[it])
        copies += col_copies(2 + 2 * it, lambda d: col_out.at[it, d], col_in.at[it], col_owner)
        for copy in copies:
            copy.start()
        return copies

    def receive(it, mine):
        for d in range(1, B):
            landed(2 + 2 * it, row_in.at[it], d, A + d)
            mine = mine + row_in[it, d]
        for d in range(A):
            landed(2 + 2 * it, col_in.at[it], d, d)
            mine = mine + col_in[it, d]
        return mine

    def wide(x):
        return jnp.broadcast_to(x[:, 0:1], (1, n))

    step_rate = 1.0 / total
    mine, _ = partials(0)
    sent = send_partials(0)
    sum0 = wide(scal_finish(0))
    mine = receive(0, mine)
    y, t = mine[0:1], mine[1:2]
    stay = 1.0 - step_rate * (0.5 * total + 0.5 * t)
    grown0 = step_rate * (0.5 * sum0 + 0.5 * y) + weights0 * stay
    grown[...] = grown0
    seconds = row_copies(3, lambda d: grown, row_w.at[1]) + col_copies(3, lambda d: grown, col_w.at[1], col_user)
    for copy in seconds:
        copy.start()

    row_acc[0] = jnp.zeros((B, n, 128), f32)
    col_acc[...] = jnp.zeros_like(col_acc)
    weigh_row(0, grown0)
    weigh_col(own, grown0)

    def arrive_second(m):
        @pl.when(m < A)
        def _():
            o = place(m)
            landed(3, col_w.at[1], o, o)
            weigh_col(o, col_w[1, o])

        @pl.when((m < B) & (m > 0))
        def _():
            landed(3, row_w.at[1], m, A + m)
            weigh_row(m, row_w[1, m])

    units(False, lambda m: None, arrive_second, lambda: scal_start(1, lanes(grown0)))

    sum1 = wide(scal_finish(1))
    mine, everything = partials(1)
    sent += send_partials(1)
    base = step_rate * (0.5 * sum1) + grown0 * stay
    scal_start(2, lanes(base + (0.5 * step_rate) * everything))
    first_change = lanes(jnp.abs(grown0 / sum1 - weights0 / sum0))
    mine = receive(1, mine)
    grown1 = base + (0.5 * step_rate) * mine[0:1]
    sum2 = wide(scal_finish(2))
    final = grown1 / sum2
    second_change = lanes(jnp.abs(final - grown0 / sum1))
    lane = lax.broadcasted_iota(jnp.int32, (1, 128), 1)
    scal_start(3, jnp.where(lane == 0, first_change, second_change))
    dist_ref[...] = (total * final).reshape(n)
    both = scal_finish(3)
    res_ref[0] = jnp.sum(jnp.where(lane == 0, both, 0.0))
    res_ref[1] = jnp.sum(jnp.where(lane == 1, both, 0.0))

    for copy in feat_rows + start_rows + start_cols + seconds + sent + [to_sibling]:
        copy.wait_send()

    @pl.when(can_up)
    def _():
        own_up.wait_send()

    @pl.when(can_down)
    def _():
        own_down.wait_send()

    for o in others[1:]:
        pass_on(o, lambda copy: copy.wait_send())


def on_device(A, B, features, initial):
    feats, n = features.shape
    devices = 2 * A * B
    vmem = lambda *shape: pltpu.VMEM(shape, f32)
    dist, res = pl.pallas_call(
        functools.partial(kernel, A, B),
        out_shape=(jax.ShapeDtypeStruct((n,), f32), jax.ShapeDtypeStruct((2,), f32)),
        in_specs=[pl.BlockSpec(memory_space=pltpu.VMEM)] * 2,
        out_specs=(pl.BlockSpec(memory_space=pltpu.VMEM), pl.BlockSpec(memory_space=pltpu.SMEM)),
        scratch_shapes=[
            vmem(A, feats, n), vmem(B, feats, n), vmem(2, A, 1, n), vmem(2, B, 1, n),
            vmem(2, A, 2, n), vmem(2, B, 2, n), vmem(2, A, 2, n), vmem(2, B, 2, n), vmem(1, n),
            pltpu.VMEM((B, n, 4 * feats), bf16), pltpu.VMEM((A + 1, 4 * feats, n), bf16),
            pltpu.VMEM((B, 16, n), bf16), vmem(A + 1, 1, n),
            pltpu.VMEM((A * B + 1, n, n), bf16),
            vmem(2, B, n, 128), vmem(A + 1, 16, n), vmem(4, devices, 1, 128),
            pltpu.SemaphoreType.DMA((5, A + B + 2)), pltpu.SemaphoreType.DMA((5, A + B)),
            pltpu.SemaphoreType.DMA((4,)), pltpu.SemaphoreType.DMA((4,)),
        ],
        compiler_params=pltpu.CompilerParams(
            collective_id=0, has_side_effects=True, vmem_limit_bytes=56 * 1024 * 1024
        ),
    )(features, initial.reshape(1, n))
    return dist, res


def solution(mesh):
    rows = mesh.shape["row"]
    B = 1
    while 4 * B * B <= rows:
        B *= 2
    A = rows // B
    placed = (P(None, ("row", "col")), P(("row", "col")))
    return jax.shard_map(
        functools.partial(on_device, A, B), mesh=mesh, in_specs=placed,
        out_specs=(P(("row", "col")), P()), check_vma=False,
    )
```

```python
import functools

import jax
import jax.numpy as jnp
from jax import lax
from jax.experimental import pallas as pl
from jax.experimental.pallas import tpu as pltpu
from jax.sharding import PartitionSpec as P

intensity = 0.25
ROW_TILE = 256
MESH_ID = pl.DeviceIdType.MESH
f32, bf16 = jnp.float32, jnp.bfloat16


def split3(x):
    hi = x.astype(bf16).astype(f32)
    mid = (x - hi).astype(bf16).astype(f32)
    return hi, mid, (x - hi - mid).astype(bf16).astype(f32)


def weight_rows(w, count):
    shape = (count, w.shape[1])
    hi, mid, low = (jnp.broadcast_to(v, shape) for v in split3(w))
    at = lax.broadcasted_iota(jnp.int32, shape, 0)
    tail = jnp.where(at == 3, 1.0, 0.0).astype(f32)
    return jnp.where(at == 0, hi, jnp.where(at == 1, mid, jnp.where(at == 2, low, tail)))


def kernel(
    A, B, feat_ref, init_ref, dist_ref, res_ref,
    col_feat, row_feat, col_w, row_w, col_in, row_in, col_out, row_out, grown,
    row_op, col_op, left, right, kept, row_acc, col_acc, scal,
    send_sem, recv_sem, scal_send, scal_recv,
):
    half = feat_ref.shape[0] // 2
    n = feat_ref.shape[1]
    devices = 2 * A * B
    total = n * devices
    row, core = lax.axis_index("row"), lax.axis_index("col")
    me = row * 2 + core
    p, q = lax.div(row, B), lax.rem(row, B)
    tile = min(ROW_TILE, n)
    own = A

    def later(x, y):
        return jnp.where(x > y, 1, 0)

    row_partner = [None] + [(p * B + (q ^ d), core) for d in range(1, B)]
    others = [p] + [lax.rem(p + d, A) for d in range(1, A)]
    col_user = [(row, 1 - core)] + [(o * B + q, core ^ later(p, o)) for o in others[1:]]
    col_owner = [(row, 1 - core)] + [(o * B + q, core ^ later(o, p)) for o in others[1:]]

    def copy_to(round_id, src, dst, send_slot, recv_slot, device):
        return pltpu.make_async_remote_copy(
            src_ref=src, dst_ref=dst, send_sem=send_sem.at[round_id, send_slot],
            recv_sem=recv_sem.at[round_id, recv_slot], device_id=device, device_id_type=MESH_ID,
        )

    def row_copies(round_id, src, dst):
        return [
            copy_to(round_id, src(d), dst.at[d], A + d, A + d, row_partner[d]) for d in range(1, B)
        ]

    def col_copies(round_id, src, dst, to):
        return [copy_to(round_id, src(d), dst.at[p], d, p, to[d]) for d in range(A)]

    def landed(round_id, dst, slot, sem_slot):
        copy_to(round_id, dst.at[slot], dst.at[slot], sem_slot, sem_slot, (row, 1 - core)).wait_recv()

    can_up, can_down = p < A - 1, p > 0
    up, down_at = ((p + 1) * B + q, core), ((p - 1) * B + q, core)
    own_up = copy_to(0, feat_ref, col_feat.at[p], A + B, p, up)
    own_down = copy_to(0, feat_ref, col_feat.at[p], A + B + 1, p, ((p - 1) * B + q, 1 - core))
    to_sibling = copy_to(0, feat_ref, col_feat.at[p], p, p, (row, 1 - core))

    def pass_on(o, act):
        @pl.when((o < p) & can_up)
        def _():
            act(copy_to(0, col_feat.at[o], col_feat.at[o], o, o, up))

        @pl.when((o > p) & can_down)
        def _():
            act(copy_to(0, col_feat.at[o], col_feat.at[o], o, o, down_at))

    def at_distance(m):
        above = A - 1 - p
        near = jnp.minimum(p, above)
        step = lax.div(m + 1, 2)
        mixed = jnp.where(lax.rem(m, 2) == 1, p - step, p + step)
        rest = jnp.where(above > p, p + m - near, p - m + near)
        return jnp.where(m <= 2 * near, mixed, rest)

    def all_others(act):
        if devices <= 64:
            for k in range(1, devices):
                act((row ^ (k // 2), core ^ (k % 2)))
        else:
            def one(k, carry):
                act((row ^ lax.div(k, 2), core ^ lax.rem(k, 2)))
                return carry

            lax.fori_loop(1, devices, one, 0)

    def scal_start(round_id, value):
        scal[round_id, me] = value
        all_others(lambda device: pltpu.make_async_remote_copy(
            src_ref=scal.at[round_id, me], dst_ref=scal.at[round_id, me], send_sem=scal_send.at[round_id],
            recv_sem=scal_recv.at[round_id], device_id=device, device_id_type=MESH_ID,
        ).start())

    def scal_finish(round_id):
        every = scal.at[round_id, pl.ds(0, devices - 1)]
        copy = pltpu.make_async_remote_copy(
            src_ref=every, dst_ref=every, send_sem=scal_send.at[round_id],
            recv_sem=scal_recv.at[round_id], device_id=(row, 1 - core), device_id_type=MESH_ID,
        )
        copy.wait_recv()
        copy.wait_send()
        return jnp.sum(scal[round_id], axis=0)

    def lanes(x):
        return jnp.broadcast_to(jnp.sum(x, axis=1, keepdims=True), (1, 128))

    def prepare_row(slot, f):
        g = jnp.concatenate([f[half:], -f[:half]], axis=0) * (0.5 * intensity)
        hi = g.astype(bf16).astype(f32)
        both = jnp.concatenate([hi, g - hi], axis=0)
        x = both.T.astype(bf16)
        row_op[slot] = jnp.concatenate([x, x], axis=1)

    def prepare_col(slot, f):
        hi = f.astype(bf16)
        low = (f - hi.astype(f32)).astype(bf16)
        col_op[slot] = jnp.concatenate([hi, hi, low, low], axis=0)

    def weigh_row(slot, w):
        left[slot] = weight_rows(w, 16).astype(bf16)

    def weigh_col(slot, w):
        right[slot] = w

    barrier = pltpu.get_barrier_semaphore()

    all_others(lambda device: pl.semaphore_signal(
        barrier, inc=1, device_id=device, device_id_type=MESH_ID
    ))

    weights0 = init_ref[...]
    row_acc[...] = jnp.zeros_like(row_acc)
    col_acc[...] = jnp.zeros_like(col_acc)
    prepare_row(0, feat_ref[...])
    prepare_col(own, feat_ref[...])
    weigh_row(0, weights0)
    weigh_col(own, weights0)
    pl.semaphore_wait(barrier, devices - 1)

    to_sibling.start()

    @pl.when(can_up)
    def _():
        own_up.start()

    @pl.when(can_down)
    def _():
        own_down.start()

    feat_rows = row_copies(0, lambda d: feat_ref, row_feat)
    start_rows = row_copies(1, lambda d: init_ref, row_w.at[0])
    start_cols = col_copies(1, lambda d: init_ref, col_w.at[0], col_user)
    for copy in feat_rows + start_rows + start_cols:
        copy.start()
    def unit(first, kept_slot, row_slot, col_slot, scale):
        down = jnp.zeros((16, n), f32)
        across_w = jnp.broadcast_to(right[col_slot], (8, n))
        for r in range(n // tile):
            at = pl.ds(r * tile, tile)
            if first:
                payoff = jnp.dot(row_op[row_slot, at], col_op[col_slot], preferred_element_type=f32)
                t = jnp.tanh(payoff.astype(bf16))
                kept[kept_slot, at] = t
            else:
                t = kept[kept_slot, at]
            wide_t = t.astype(f32)
            weighed = jnp.zeros((tile, 128), f32)
            plain = jnp.zeros((tile, 128), f32)
            for k in range(n // 128):
                part = wide_t[:, k * 128:(k + 1) * 128]
                by = across_w[:, k * 128:(k + 1) * 128]
                weighed += (part.reshape(tile // 8, 8, 128) * by[None]).reshape(tile, 128)
                if first:
                    plain += part
            row_acc[0, row_slot, at] += weighed if scale is None else scale * weighed
            if first:
                row_acc[1, row_slot, at] += plain if scale is None else scale * plain
            down += jnp.dot(left[row_slot, :, r * tile:(r + 1) * tile], t, preferred_element_type=f32)
        col_acc[col_slot] += down if scale is None else scale * down

    def units(first, land, arrive, between):
        def near(j, carry):
            @pl.when(j == 1)
            def _():
                land(0)
                arrive(0)

            unit(first, jnp.where(j == 0, 0, A * B), 0, jnp.where(j == 0, own, p), 0.5)
            return carry

        lax.fori_loop(0, 2, near, 0)
        between()

        def shell(m, carry):
            @pl.when((m == 1) | jnp.logical_not(can_up & can_down))
            def _():
                land(m)

            arrive(m)

            def one(j, carry):
                dq = jnp.where(j <= m, m, j - m - 1)
                dp = jnp.where(j <= m, j, m)
                own_or_sibling = jnp.where((q ^ dq) > q, p, own)
                col_slot = jnp.where(dp == 0, own_or_sibling, at_distance(jnp.maximum(dp, 1)))

                @pl.when((j == m) & (m < max(A, B) - 1) & can_up & can_down)
                def _():
                    land(m + 1)

                def run():
                    unit(first, dq * A + dp, dq, col_slot, None)

                if A == B:
                    run()
                else:
                    pl.when((dq < B) & (dp < A))(run)
                return carry

            return lax.fori_loop(0, 2 * m + 1, one, carry)

        lax.fori_loop(1, max(A, B), shell, 0)


    def place(m):
        return jnp.where(m == 0, p, at_distance(jnp.maximum(m, 1)))

    def land_first(m):
        @pl.when(m < A)
        def _():
            o = place(m)
            landed(0, col_feat, o, o)
            pass_on(o, lambda copy: copy.start())

    def arrive_first(m):
        @pl.when(m < A)
        def _():
            o = place(m)
            landed(1, col_w.at[0], o, o)
            prepare_col(o, col_feat[o])
            weigh_col(o, col_w[0, o])

        @pl.when((m < B) & (m > 0))
        def _():
            landed(0, row_feat, m, A + m)
            landed(1, row_w.at[0], m, A + m)
            prepare_row(m, row_feat[m])
            weigh_row(m, row_w[0, m])

    units(True, land_first, arrive_first, lambda: scal_start(0, lanes(weights0)))

    def partials(it):
        def of_row(d):
            y = jnp.sum(row_acc[0, d].T, axis=0, keepdims=True)
            t = jnp.sum(row_acc[1, d].T, axis=0, keepdims=True) if it == 0 else jnp.zeros((1, n), f32)
            return -y, t

        def of_col(acc):
            return acc[0:1] + acc[1:2] + acc[2:3], -acc[3:4]

        everything = jnp.zeros((1, n), f32)
        for d in range(1, B):
            y, t = of_row(d)
            row_out[it, d] = jnp.concatenate([y, t], axis=0)
            everything += y
        for d in range(A):
            y, t = of_col(col_acc[others[d]])
            col_out[it, d] = jnp.concatenate([y, t], axis=0)
            everything += y
        y0, t0 = of_row(0)
        y1, t1 = of_col(col_acc[own])
        mine = jnp.concatenate([y0 + y1, t0 + t1], axis=0)
        return mine, everything + y0 + y1

    def send_partials(it):
        copies = row_copies(2 + 2 * it, lambda d: row_out.at[it, d], row_in.at[it])
        copies += col_copies(2 + 2 * it, lambda d: col_out.at[it, d], col_in.at[it], col_owner)
        for copy in copies:
            copy.start()
        return copies

    def receive(it, mine):
        for d in range(1, B):
            landed(2 + 2 * it, row_in.at[it], d, A + d)
            mine = mine + row_in[it, d]
        for d in range(A):
            landed(2 + 2 * it, col_in.at[it], d, d)
            mine = mine + col_in[it, d]
        return mine

    def wide(x):
        return jnp.broadcast_to(x[:, 0:1], (1, n))

    step_rate = 1.0 / total
    mine, _ = partials(0)
    sent = send_partials(0)
    sum0 = wide(scal_finish(0))
    mine = receive(0, mine)
    y, t = mine[0:1], mine[1:2]
    stay = 1.0 - step_rate * (0.5 * total + 0.5 * t)
    grown0 = step_rate * (0.5 * sum0 + 0.5 * y) + weights0 * stay
    grown[...] = grown0
    seconds = row_copies(3, lambda d: grown, row_w.at[1]) + col_copies(3, lambda d: grown, col_w.at[1], col_user)
    for copy in seconds:
        copy.start()

    row_acc[0] = jnp.zeros((B, n, 128), f32)
    col_acc[...] = jnp.zeros_like(col_acc)
    weigh_row(0, grown0)
    weigh_col(own, grown0)

    def arrive_second(m):
        @pl.when(m < A)
        def _():
            o = place(m)
            landed(3, col_w.at[1], o, o)
            weigh_col(o, col_w[1, o])

        @pl.when((m < B) & (m > 0))
        def _():
            landed(3, row_w.at[1], m, A + m)
            weigh_row(m, row_w[1, m])

    units(False, lambda m: None, arrive_second, lambda: scal_start(1, lanes(grown0)))

    sum1 = wide(scal_finish(1))
    mine, everything = partials(1)
    sent += send_partials(1)
    base = step_rate * (0.5 * sum1) + grown0 * stay
    scal_start(2, lanes(base + (0.5 * step_rate) * everything))
    first_change = lanes(jnp.abs(grown0 / sum1 - weights0 / sum0))
    mine = receive(1, mine)
    grown1 = base + (0.5 * step_rate) * mine[0:1]
    sum2 = wide(scal_finish(2))
    final = grown1 / sum2
    second_change = lanes(jnp.abs(final - grown0 / sum1))
    lane = lax.broadcasted_iota(jnp.int32, (1, 128), 1)
    scal_start(3, jnp.where(lane == 0, first_change, second_change))
    dist_ref[...] = (total * final).reshape(n)
    both = scal_finish(3)
    res_ref[0] = jnp.sum(jnp.where(lane == 0, both, 0.0))
    res_ref[1] = jnp.sum(jnp.where(lane == 1, both, 0.0))

    for copy in feat_rows + start_rows + start_cols + seconds + sent + [to_sibling]:
        copy.wait_send()

    @pl.when(can_up)
    def _():
        own_up.wait_send()

    @pl.when(can_down)
    def _():
        own_down.wait_send()

    for o in others[1:]:
        pass_on(o, lambda copy: copy.wait_send())


def on_device(A, B, features, initial):
    feats, n = features.shape
    devices = 2 * A * B
    vmem = lambda *shape: pltpu.VMEM(shape, f32)
    dist, res = pl.pallas_call(
        functools.partial(kernel, A, B),
        out_shape=(jax.ShapeDtypeStruct((n,), f32), jax.ShapeDtypeStruct((2,), f32)),
        in_specs=[pl.BlockSpec(memory_space=pltpu.VMEM)] * 2,
        out_specs=(pl.BlockSpec(memory_space=pltpu.VMEM), pl.BlockSpec(memory_space=pltpu.SMEM)),
        scratch_shapes=[
            vmem(A, feats, n), vmem(B, feats, n), vmem(2, A, 1, n), vmem(2, B, 1, n),
            vmem(2, A, 2, n), vmem(2, B, 2, n), vmem(2, A, 2, n), vmem(2, B, 2, n), vmem(1, n),
            pltpu.VMEM((B, n, 4 * feats), bf16), pltpu.VMEM((A + 1, 4 * feats, n), bf16),
            pltpu.VMEM((B, 16, n), bf16), vmem(A + 1, 1, n),
            pltpu.VMEM((A * B + 1, n, n), bf16),
            vmem(2, B, n, 128), vmem(A + 1, 16, n), vmem(4, devices, 1, 128),
            pltpu.SemaphoreType.DMA((5, A + B + 2)), pltpu.SemaphoreType.DMA((5, A + B)),
            pltpu.SemaphoreType.DMA((4,)), pltpu.SemaphoreType.DMA((4,)),
        ],
        compiler_params=pltpu.CompilerParams(
            collective_id=0, has_side_effects=True, vmem_limit_bytes=56 * 1024 * 1024
        ),
    )(features, initial.reshape(1, n))
    return dist, res


def solution(mesh):
    rows = mesh.shape["row"]
    B = 1
    while 4 * B * B <= rows:
        B *= 2
    A = rows // B
    placed = (P(None, ("row", "col")), P(("row", "col")))
    return jax.shard_map(
        functools.partial(on_device, A, B), mesh=mesh, in_specs=placed,
        out_specs=(P(("row", "col")), P()), check_vma=False,
    )
```
